32 devices in a mesh: user: 4 (over y, core), item: 8 (over z, x).
Axes of the slice: x: 2, y: 2, z: 4, core: 2. Of those that a mesh axis runs over, the one named last changes fastest.
Arguments:
- users: bfloat16 [4096, 256], P('user'), may hold values from -40 to 40
- catalog_vectors: bfloat16 [65536, 256], P('item'), may hold values from -8 to 8
- positives: int32 [4096], P('user'), may hold values from 0 to 65535
Outputs:
- loss: float32 [4096], P('user')
- user_grad: bfloat16 [4096, 256], P('user')
- item_grad: bfloat16 [65536, 256], P(('item', 'user'))
The draws below stay inside these ranges and needn't reach their ends.
All inputs are finite; a program needn't handle non-finite values.
Results may differ from the reference program's by a relative error of at most 0.0034.
Values may be sent and summed in bfloat16 or wider, within the bound.
A program may use at most 64 MiB of HBM per device.

```python
import math
import jax
import jax.numpy as jnp
from jax import lax

E = 256
USER_DEV = 1024
USERS = 4096
ITEMS = 65536
N_USER = 4


def shared_draw(key):
    item_key = jax.random.fold_in(key, 11)
    user_key = jax.random.fold_in(key, 12)
    sign_key = jax.random.fold_in(key, 14)
    item_vals = jnp.clip(jax.random.normal(item_key, (ITEMS, E), jnp.float32), -6.0, 6.0)
    user_vals = jnp.clip(jax.random.normal(user_key, (USERS, E), jnp.float32), -6.0, 6.0)
    signs = jnp.where(jax.random.bernoulli(sign_key, 0.5, (6, E)), 1.0, -1.0).astype(jnp.float32)
    targets = [110.0, 160.0, 230.0, 110.0, 160.0, 230.0]
    for number in range(6):
        target_score = targets[number]
        item_row = number * (ITEMS // 7) % ITEMS
        partner = (item_row + 1) % ITEMS
        user_row = number * (USERS // 6) % USERS
        base_row = 2.0 * signs[number]
        item_vals = item_vals.at[item_row].set(base_row)
        item_vals = item_vals.at[partner].set(base_row * (1.0 - 2.5 / target_score))
        user_vals = user_vals.at[user_row].set(signs[number] * (target_score * 2.0 / E))
    return (user_vals, item_vals)


def draw_users(key, part):
    user_vals, item_vals = shared_draw(key)
    return user_vals.astype(jnp.bfloat16)


def draw_catalog_vectors(key, part):
    user_vals, item_vals = shared_draw(key)
    return item_vals.astype(jnp.bfloat16)


def place_ends(drawn, own_key, low, largest):
    longest = drawn.shape.index(max(drawn.shape))
    spots = []
    for shift in (0, 1):
        where = [jax.random.randint(jax.random.fold_in(own_key, axis), (), 0, length) for axis, length in enumerate(drawn.shape)]
        where[longest] = (where[longest] + shift) % drawn.shape[longest]
        spots.append(tuple(where))
    return drawn.at[spots[0]].set(low).at[spots[1]].set(largest)


def setup_inputs(seed: int = 0) -> dict:
    key_list = jax.random.split(jax.random.key(seed), 4)
    users = draw_users(jax.random.fold_in(key_list[3], 71), 0)
    catalog_vectors = draw_catalog_vectors(jax.random.fold_in(key_list[3], 71), 0)
    positives = place_ends(jax.random.randint(key_list[2], (USERS,), 0, ITEMS), jax.random.fold_in(key_list[2], 1), 0, ITEMS - 1).astype(jnp.int32)
    return {"users": users, "catalog_vectors": catalog_vectors, "positives": positives}


sharpness_divisor = 4.0


def reference(users, catalog_vectors, positives):
    count = catalog_vectors.shape[0]
    width = catalog_vectors.shape[1]
    row_block = math.gcd(USER_DEV, 256)
    item_index = lax.broadcasted_iota(jnp.int32, (1, count), 1)

    def shard_step(total, index):
        user_shard = lax.dynamic_slice_in_dim(users, (index * USER_DEV).astype(jnp.int32), USER_DEV, 0)
        pos_shard = lax.dynamic_slice_in_dim(positives, (index * USER_DEV).astype(jnp.int32), USER_DEV, 0)
        user_blocks = user_shard.reshape(USER_DEV // row_block, row_block, width)
        pos_blocks = pos_shard.reshape(USER_DEV // row_block, row_block)

        def row_step(accumulated_sum, inputs):
            customer_vector_list, pos_rows = inputs
            affinity_grid = jnp.dot(customer_vector_list, catalog_vectors.T, preferred_element_type=jnp.float32) / sharpness_divisor
            top = jnp.max(affinity_grid, axis=1)
            lse = top + jnp.log(jnp.sum(jnp.exp(affinity_grid - top[:, None]), axis=1))
            positive_indicator = item_index == pos_rows[:, None]
            pos_score = jnp.sum(jnp.where(positive_indicator, affinity_grid, 0.0), axis=1)
            normalized_probabilities = (jnp.exp(affinity_grid - lse[:, None]) - positive_indicator.astype(jnp.float32)).astype(jnp.bfloat16)
            customer_fraction = jnp.dot(normalized_probabilities, catalog_vectors, preferred_element_type=jnp.float32) / sharpness_divisor
            accumulated_sum = accumulated_sum + jnp.dot(normalized_probabilities.T, customer_vector_list, preferred_element_type=jnp.float32)
            return accumulated_sum, (lse - pos_score, customer_fraction.astype(jnp.bfloat16))

        accumulated_sum, (losses, user_parts) = lax.scan(row_step, jnp.zeros((count, width), jnp.float32), (user_blocks, pos_blocks))
        return total + accumulated_sum / sharpness_divisor, (losses.reshape(-1), user_parts.reshape(-1, width))

    total, (losses, user_parts) = lax.scan(shard_step, jnp.zeros((count, width), jnp.float32), jnp.arange(N_USER, dtype=jnp.int32))
    return losses.reshape(-1), user_parts.reshape(-1, width), total.astype(jnp.bfloat16)
```

```python
import functools
import math

import jax
import jax.numpy as jnp
from jax import lax
from jax.experimental import pallas as pl
from jax.experimental.pallas import tpu as pltpu
from jax.sharding import PartitionSpec as P

sharpness_divisor = 4.0
inverse = 1.0 / sharpness_divisor
to_log2 = math.log2(math.e) / sharpness_divisor
MESH = pl.DeviceIdType.MESH


def kernel(
    n_item, step, tile, lanes,
    users_ref, items_ref, pos_ref,
    loss_ref, user_out, item_out,
    grown, score_a, score_b, tops, top, total, hits, stat_out, stat_in, hit_out, hit_in, factor,
    weight_a, weight_b, own_part, core_out, core_in, y_out, y_in, kept, user_sum,
    part_out, part_in, done, stat_sems, hit_sems, core_sems, y_sems, part_sems, done_sems,
):
    rows, width = users_ref.shape
    count = items_ref.shape[0]
    nstep = count // step
    own = count // 4
    per_block = own // step
    piece = width // n_item
    u = lax.axis_index("user")
    me = lax.axis_index("item")
    core = lax.rem(u, 2)
    y = u // 2
    core_peer = {"user": 2 * y + 1 - core, "item": me}
    y_peer = {"user": 2 * (1 - y) + core, "item": me}

    def item_peer(d):
        return {"user": u, "item": lax.rem(me + d, n_item)}

    barrier = pltpu.get_barrier_semaphore()
    for peer in [core_peer, y_peer] + [item_peer(d) for d in range(1, n_item)]:
        pl.semaphore_signal(barrier, inc=1, device_id=peer, device_id_type=MESH)

    top[...] = jnp.full_like(top, -jnp.inf)
    total[...] = jnp.zeros_like(total)
    hits[...] = jnp.zeros_like(hits)
    user_sum[...] = jnp.zeros_like(user_sum)
    groups = tile // 8
    first_row = lax.broadcasted_iota(jnp.int32, (groups, 1, 1), 0) * 8
    sublane = lax.broadcasted_iota(jnp.int32, (8, lanes), 0)
    offset = me * count

    def score(number, out):
        piece_rows = items_ref[pl.ds(pl.multiple_of(number * step, step), step), :]
        out[...] = lax.dot_general(
            piece_rows, users_ref[...], (((1,), (1,)), ((), ())),
            preferred_element_type=jnp.float32,
        )

    def grow(number, source):
        for t in range(step // tile):
            start = pl.multiple_of(number * step + t * tile, tile)
            for k in range(rows // lanes):
                cols = slice(k * lanes, (k + 1) * lanes)
                s = source[t * tile:(t + 1) * tile, cols].reshape(groups, 8, lanes)
                old = top[:, cols]
                new = jnp.maximum(old, jnp.max(s, axis=0))
                e = jnp.exp2((s - new[None]) * to_log2)
                grown[pl.ds(start, tile), cols] = e.reshape(tile, lanes)
                top[:, cols] = new
                tops[number * (step // tile) + t, :, cols] = new
                total[:, cols] = total[:, cols] * jnp.exp2((old - new) * to_log2) + jnp.sum(e, axis=0)
                rel = pos_ref[:, cols] - (offset + start) - sublane
                hits[:, cols] += jnp.sum(jnp.where(rel[None] == first_row, s, 0.0), axis=0)

    score(0, score_a)

    @pl.loop(0, nstep // 2)
    def _(i):
        score(2 * i + 1, score_b)
        grow(2 * i, score_a)
        score(jnp.minimum(2 * i + 2, nstep - 1), score_a)
        grow(2 * i + 1, score_b)

    m8 = top[...]
    m1 = jnp.max(m8, axis=0, keepdims=True)
    l1 = jnp.sum(total[...] * jnp.exp2((m8 - m1) * to_log2), axis=0, keepdims=True)
    p1 = jnp.sum(hits[...], axis=0, keepdims=True)
    stat_out[0:1, :] = m1
    stat_out[1:2, :] = l1
    hit_out[...] = p1
    pl.semaphore_wait(barrier, n_item + 1)
    stat_copies, hit_copies = [], []
    for d in range(1, n_item):
        stat_copies.append(pltpu.make_async_remote_copy(
            src_ref=stat_out, dst_ref=stat_in.at[d - 1], send_sem=stat_sems.at[0, d - 1],
            recv_sem=stat_sems.at[1, d - 1], device_id=item_peer(d), device_id_type=MESH))
        stat_copies[-1].start()
    for d in range(1, n_item):
        hit_copies.append(pltpu.make_async_remote_copy(
            src_ref=hit_out, dst_ref=hit_in.at[d - 1], send_sem=hit_sems.at[0, d - 1],
            recv_sem=hit_sems.at[1, d - 1], device_id=item_peer(d), device_id_type=MESH))
        hit_copies[-1].start()
    for copy in stat_copies:
        copy.wait()
    all_top = m1
    for d in range(n_item - 1):
        all_top = jnp.maximum(all_top, stat_in[d, 0:1, :])
    all_sum = l1 * jnp.exp2((m1 - all_top) * to_log2)
    for d in range(n_item - 1):
        all_sum = all_sum + stat_in[d, 1:2, :] * jnp.exp2((stat_in[d, 0:1, :] - all_top) * to_log2)
    loss_ref[...] = all_top * inverse + jnp.log(all_sum)
    factor[0:1, :] = all_top
    factor[1:2, :] = 1.0 / all_sum

    def weigh(start, out):
        for t in range(step // tile):
            begin = pl.multiple_of(start + t * tile, tile)
            for k in range(rows // lanes):
                cols = slice(k * lanes, (k + 1) * lanes)
                f = jnp.exp2((tops[begin // tile, :, cols] - factor[0:1, cols]) * to_log2) * factor[1:2, cols]
                w = grown[pl.ds(begin, tile), cols].reshape(groups, 8, lanes) * f[None]
                rel = pos_ref[:, cols] - (offset + begin) - sublane
                w = jnp.where(rel[None] == first_row, w - 1.0, w)
                out[t * tile:(t + 1) * tile, cols] = w.reshape(tile, lanes).astype(jnp.bfloat16)

    def item_part(weight):
        return jnp.dot(weight[...], users_ref[...], preferred_element_type=jnp.float32) * inverse

    def user_part(start, weight):
        return lax.dot_general(
            items_ref[pl.ds(start, step), :], weight[...], (((0,), (0,)), ((), ())),
            preferred_element_type=jnp.float32,
        )

    def core_copy(q):
        return pltpu.make_async_remote_copy(
            src_ref=core_out.at[q], dst_ref=core_in.at[q], send_sem=core_sems.at[0, q],
            recv_sem=core_sems.at[1, q], device_id=core_peer, device_id_type=MESH)

    def y_copy(q):
        return pltpu.make_async_remote_copy(
            src_ref=y_out.at[q], dst_ref=y_in.at[q], send_sem=y_sems.at[0, q],
            recv_sem=y_sems.at[1, q], device_id=y_peer, device_id_type=MESH)

    def settle(q):
        core_copy(q).wait_recv()
        both = own_part[q % 2] + core_in[q].astype(jnp.float32)

        @pl.when(q < per_block)
        def _():
            y_out[q % per_block] = both.astype(jnp.bfloat16)
            y_copy(q % per_block).start()

        @pl.when(q >= per_block)
        def _():
            kept[q % per_block] = both

    @pl.loop(0, 2 * per_block)
    def _(q):
        far = 1 - q // per_block
        block_y = lax.rem(y + far, 2)
        inner = lax.rem(q, per_block) * step
        start_a = pl.multiple_of((2 * block_y + 1 - core) * own + inner, step)
        start_b = pl.multiple_of((2 * block_y + core) * own + inner, step)
        weigh(start_a, weight_a)
        core_out[q] = item_part(weight_a).astype(jnp.bfloat16)
        weigh(start_b, weight_b)
        part_a = user_part(start_a, weight_a)
        core_copy(q).start()
        own_part[q % 2] = item_part(weight_b)
        user_sum[...] += part_a + user_part(start_b, weight_b)

        @pl.when(q >= 1)
        def _():
            settle(q - 1)

    part_out[...] = (user_sum[...] * inverse).astype(jnp.bfloat16).reshape(part_out.shape)
    part_copies = []
    for d in range(1, n_item):
        part_copies.append(pltpu.make_async_remote_copy(
            src_ref=part_out.at[lax.rem(me + d, n_item)], dst_ref=part_in.at[d - 1],
            send_sem=part_sems.at[0, d - 1], recv_sem=part_sems.at[1, d - 1],
            device_id=item_peer(d), device_id_type=MESH))
        part_copies[-1].start()
    settle(2 * per_block - 1)
    for copy in hit_copies:
        copy.wait()
    p_all = p1
    for d in range(n_item - 1):
        p_all = p_all + hit_in[d]
    loss_ref[...] = loss_ref[...] - p_all * inverse
    mine = user_sum[pl.ds(pl.multiple_of(me * piece, piece), piece), :] * inverse
    for d in range(n_item - 1):
        part_copies[d].wait()
        mine = mine + part_in[d].astype(jnp.float32)
    done[me] = mine.astype(jnp.bfloat16)
    done_copies = []
    for d in range(1, n_item):
        done_copies.append(pltpu.make_async_remote_copy(
            src_ref=done.at[me], dst_ref=done.at[me],
            send_sem=done_sems.at[0, d - 1], recv_sem=done_sems.at[1, d - 1],
            device_id=item_peer(d), device_id_type=MESH))
        done_copies[-1].start()
    for q in range(per_block):
        y_copy(q).wait()
        item_out[q * step:(q + 1) * step, :] = (kept[q] + y_in[q].astype(jnp.float32)).astype(jnp.bfloat16)
    for q in range(2 * per_block):
        core_copy(q).wait_send()
    for copy in done_copies:
        copy.wait()
    user_out[...] = done[...].reshape(user_out.shape)


def solution(mesh):
    n_item = mesh.shape["item"]
    assert mesh.shape["user"] == 4

    def per_device(users, catalog_vectors, positives):
        rows, width = users.shape
        count = catalog_vectors.shape[0]
        own = count // 4
        step, tile, lanes = min(512, own), 256, 128
        per_block = own // step
        piece = width // n_item
        f32, bf16 = jnp.float32, jnp.bfloat16
        vmem = pl.BlockSpec(memory_space=pltpu.VMEM)
        dma = pltpu.SemaphoreType.DMA
        loss, user_t, item_grad = pl.pallas_call(
            functools.partial(kernel, n_item, step, tile, lanes),
            out_shape=(
                jax.ShapeDtypeStruct((1, rows), f32),
                jax.ShapeDtypeStruct((width, rows), bf16),
                jax.ShapeDtypeStruct((own, width), bf16),
            ),
            in_specs=[vmem] * 3,
            out_specs=(vmem,) * 3,
            scratch_shapes=[
                pltpu.VMEM((count, rows), f32),
                pltpu.VMEM((step, rows), f32),
                pltpu.VMEM((step, rows), f32),
                pltpu.VMEM((count // tile, 8, rows), f32),
                pltpu.VMEM((8, rows), f32),
                pltpu.VMEM((8, rows), f32),
                pltpu.VMEM((8, rows), f32),
                pltpu.VMEM((2, rows), f32),
                pltpu.VMEM((n_item - 1, 2, rows), f32),
                pltpu.VMEM((1, rows), f32),
                pltpu.VMEM((n_item - 1, 1, rows), f32),
                pltpu.VMEM((2, rows), f32),
                pltpu.VMEM((step, rows), bf16),
                pltpu.VMEM((step, rows), bf16),
                pltpu.VMEM((2, step, width), f32),
                pltpu.VMEM((2 * per_block, step, width), bf16),
                pltpu.VMEM((2 * per_block, step, width), bf16),
                pltpu.VMEM((per_block, step, width), bf16),
                pltpu.VMEM((per_block, step, width), bf16),
                pltpu.VMEM((per_block, step, width), f32),
                pltpu.VMEM((width, rows), f32),
                pltpu.VMEM((n_item, piece, rows), bf16),
                pltpu.VMEM((n_item - 1, piece, rows), bf16),
                pltpu.VMEM((n_item, piece, rows), bf16),
                dma((2, n_item - 1)),
                dma((2, n_item - 1)),
                dma((2, 2 * per_block)),
                dma((2, per_block)),
                dma((2, n_item - 1)),
                dma((2, n_item - 1)),
            ],
            compiler_params=pltpu.CompilerParams(
                collective_id=0, has_side_effects=True, vmem_limit_bytes=63 * 1024 * 1024,
            ),
        )(users, catalog_vectors, positives.reshape(1, rows))
        return loss.reshape(rows), user_t.T, item_grad

    in_specs = (P("user", None), P("item", None), P("user"))
    out_specs = (P("user"), P("user", None), P(("item", "user"), None))
    return jax.shard_map(
        per_device, mesh=mesh, in_specs=in_specs, out_specs=out_specs, check_vma=False
    )
```

```python
import functools

import jax
import jax.numpy as jnp
from jax import lax
from jax.experimental import pallas as pl
from jax.experimental.pallas import tpu as pltpu
from jax.sharding import PartitionSpec as P

sharpness_divisor = 4.0
inverse = 1.0 / sharpness_divisor
MESH = pl.DeviceIdType.MESH


def kernel(
    n_item, step, tile, lanes,
    users_ref, items_ref, pos_ref,
    loss_ref, user_out, item_out,
    grown, score_a, score_b, tops, top, total, hits, stat_out, stat_in, hit_out, hit_in, factor,
    weight_a, weight_b, own_part, core_out, core_in, y_out, y_in, kept, user_sum,
    part_out, part_in, done, quarter, stat_sems, hit_sems, core_sems, y_sems, part_sems, done_sems,
):
    rows, width = users_ref.shape
    count = items_ref.shape[0]
    nstep = count // step
    own = count // 4
    per_block = own // step
    piece = width // n_item
    u = lax.axis_index("user")
    me = lax.axis_index("item")
    core = lax.rem(u, 2)
    y = u // 2
    core_peer = {"user": 2 * y + 1 - core, "item": me}
    y_peer = {"user": 2 * (1 - y) + core, "item": me}

    def item_peer(d):
        return {"user": u, "item": lax.rem(me + d, n_item)}

    barrier = pltpu.get_barrier_semaphore()
    for peer in [core_peer, y_peer] + [item_peer(d) for d in range(1, n_item)]:
        pl.semaphore_signal(barrier, inc=1, device_id=peer, device_id_type=MESH)

    top[...] = jnp.full_like(top, -jnp.inf)
    total[...] = jnp.zeros_like(total)
    hits[...] = jnp.zeros_like(hits)
    user_sum[...] = jnp.zeros_like(user_sum)
    quarter[...] = users_ref[...] * jnp.bfloat16(inverse)
    groups = tile // 8
    first_row = lax.broadcasted_iota(jnp.int32, (groups, 1, 1), 0) * 8
    sublane = lax.broadcasted_iota(jnp.int32, (8, lanes), 0)
    offset = me * count

    wide = 2 * lanes
    pieces = rows // wide

    def score(number, out, k):
        cols = slice(k * wide, (k + 1) * wide)
        piece_rows = items_ref[pl.ds(pl.multiple_of(number * step, step), step), :]
        out[:, cols] = lax.dot_general(
            piece_rows, quarter[cols, :], (((1,), (1,)), ((), ())),
            preferred_element_type=jnp.float32,
        )

    def grow(number, source, piece_number):
        for k in (2 * piece_number, 2 * piece_number + 1):
            cols = slice(k * lanes, (k + 1) * lanes)
            old, run, hit = top[:, cols], total[:, cols], hits[:, cols]
            for t in range(step // tile):
                start = pl.multiple_of(number * step + t * tile, tile)
                s = source[t * tile:(t + 1) * tile, cols].reshape(groups, 8, lanes)
                new = jnp.maximum(old, jnp.max(s, axis=0))
                e = jnp.exp(s - new[None])
                grown[pl.ds(start, tile), cols] = e.reshape(tile, lanes)
                tops[number * (step // tile) + t, :, cols] = new
                run = run * jnp.exp(old - new) + jnp.sum(e, axis=0)
                old = new
                rel = pos_ref[:, cols] - (offset + start) - sublane
                for g in range(groups):
                    hit = jnp.where(rel == 8 * g, s[g], hit)
            top[:, cols] = old
            total[:, cols] = run
            hits[:, cols] = hit

    for k in range(pieces):
        score(0, score_a, k)

    @pl.loop(0, nstep // 2)
    def _(i):
        for k in range(pieces):
            score(2 * i + 1, score_b, k)
            grow(2 * i, score_a, k)
        for k in range(pieces):
            score(jnp.minimum(2 * i + 2, nstep - 1), score_a, k)
            grow(2 * i + 1, score_b, k)

    m8 = top[...]
    m1 = jnp.max(m8, axis=0, keepdims=True)
    l1 = jnp.sum(total[...] * jnp.exp(m8 - m1), axis=0, keepdims=True)
    p1 = jnp.sum(hits[...], axis=0, keepdims=True)
    stat_out[0:1, :] = m1
    stat_out[1:2, :] = l1
    hit_out[...] = p1
    pl.semaphore_wait(barrier, n_item + 1)
    stat_copies, hit_copies = [], []
    for d in range(1, n_item):
        stat_copies.append(pltpu.make_async_remote_copy(
            src_ref=stat_out, dst_ref=stat_in.at[d - 1], send_sem=stat_sems.at[0, d - 1],
            recv_sem=stat_sems.at[1, d - 1], device_id=item_peer(d), device_id_type=MESH))
        stat_copies[-1].start()
    for d in range(1, n_item):
        hit_copies.append(pltpu.make_async_remote_copy(
            src_ref=hit_out, dst_ref=hit_in.at[d - 1], send_sem=hit_sems.at[0, d - 1],
            recv_sem=hit_sems.at[1, d - 1], device_id=item_peer(d), device_id_type=MESH))
        hit_copies[-1].start()
    for copy in stat_copies:
        copy.wait()
    all_top = m1
    for d in range(n_item - 1):
        all_top = jnp.maximum(all_top, stat_in[d, 0:1, :])
    all_sum = l1 * jnp.exp(m1 - all_top)
    for d in range(n_item - 1):
        all_sum = all_sum + stat_in[d, 1:2, :] * jnp.exp(stat_in[d, 0:1, :] - all_top)
    loss_ref[...] = all_top + jnp.log(all_sum)
    factor[0:1, :] = all_top
    factor[1:2, :] = 1.0 / all_sum

    def weigh(start, out, piece_number):
        for k in (2 * piece_number, 2 * piece_number + 1):
            cols = slice(k * lanes, (k + 1) * lanes)
            for t in range(step // tile):
                begin = pl.multiple_of(start + t * tile, tile)
                f = jnp.exp(tops[begin // tile, :, cols] - factor[0:1, cols]) * factor[1:2, cols]
                w = grown[pl.ds(begin, tile), cols].reshape(groups, 8, lanes) * f[None]
                rel = pos_ref[:, cols] - (offset + begin) - sublane
                w = jnp.where(rel[None] == first_row, w - 1.0, w)
                out[t * tile:(t + 1) * tile, cols] = w.reshape(tile, lanes).astype(jnp.bfloat16)

    def item_part(weight, t):
        return jnp.dot(
            weight[t * half:(t + 1) * half, :], users_ref[...], preferred_element_type=jnp.float32
        ) * inverse

    def user_part(start, weight, k):
        cols = slice(k * wide, (k + 1) * wide)
        user_sum[:, cols] += lax.dot_general(
            items_ref[pl.ds(start, step), :], weight[:, cols], (((0,), (0,)), ((), ())),
            preferred_element_type=jnp.float32,
        )

    def core_copy(q):
        return pltpu.make_async_remote_copy(
            src_ref=core_out.at[q], dst_ref=core_in.at[q], send_sem=core_sems.at[0, q],
            recv_sem=core_sems.at[1, q], device_id=core_peer, device_id_type=MESH)

    def y_copy(q):
        return pltpu.make_async_remote_copy(
            src_ref=y_out.at[q], dst_ref=y_in.at[q], send_sem=y_sems.at[0, q],
            recv_sem=y_sems.at[1, q], device_id=y_peer, device_id_type=MESH)

    def settle(q):
        core_copy(q).wait_recv()
        both = own_part[q % 2] + core_in[q].astype(jnp.float32)

        @pl.when(q < per_block)
        def _():
            y_out[q % per_block] = both.astype(jnp.bfloat16)
            y_copy(q % per_block).start()

        @pl.when(q >= per_block)
        def _():
            kept[q % per_block] = both

    def starts(q):
        far = 1 - q // per_block
        block_y = lax.rem(y + far, 2)
        inner = lax.rem(q, per_block) * step
        start_a = pl.multiple_of((2 * block_y + 1 - core) * own + inner, step)
        start_b = pl.multiple_of((2 * block_y + core) * own + inner, step)
        return start_a, start_b

    first = starts(0)[0]
    for k in range(pieces):
        weigh(first, weight_a, k)
    halves, half = 2, step // 2

    @pl.loop(0, 2 * per_block)
    def _(q):
        start_a, start_b = starts(q)
        next_a = starts(jnp.minimum(q + 1, 2 * per_block - 1))[0]
        for k in range(pieces):
            if k < halves:
                core_out[q, k * half:(k + 1) * half, :] = item_part(weight_a, k).astype(jnp.bfloat16)
            weigh(start_b, weight_b, k)
            user_part(start_a, weight_a, k)
        core_copy(q).start()
        for k in range(pieces):
            if k < halves:
                own_part[q % 2, k * half:(k + 1) * half, :] = item_part(weight_b, k)
            weigh(next_a, weight_a, k)
            user_part(start_b, weight_b, k)

        @pl.when(q >= 1)
        def _():
            settle(q - 1)

    part_out[...] = (user_sum[...] * inverse).astype(jnp.bfloat16).reshape(part_out.shape)
    part_copies = []
    for d in range(1, n_item):
        part_copies.append(pltpu.make_async_remote_copy(
            src_ref=part_out.at[lax.rem(me + d, n_item)], dst_ref=part_in.at[d - 1],
            send_sem=part_sems.at[0, d - 1], recv_sem=part_sems.at[1, d - 1],
            device_id=item_peer(d), device_id_type=MESH))
        part_copies[-1].start()
    settle(2 * per_block - 1)
    for copy in hit_copies:
        copy.wait()
    p_all = p1
    for d in range(n_item - 1):
        p_all = p_all + hit_in[d]
    loss_ref[...] = loss_ref[...] - p_all
    mine = user_sum[pl.ds(pl.multiple_of(me * piece, piece), piece), :] * inverse
    for d in range(n_item - 1):
        part_copies[d].wait()
        mine = mine + part_in[d].astype(jnp.float32)
    done[me] = mine.astype(jnp.bfloat16)
    done_copies = []
    for d in range(1, n_item):
        done_copies.append(pltpu.make_async_remote_copy(
            src_ref=done.at[me], dst_ref=done.at[me],
            send_sem=done_sems.at[0, d - 1], recv_sem=done_sems.at[1, d - 1],
            device_id=item_peer(d), device_id_type=MESH))
        done_copies[-1].start()
    for q in range(per_block):
        y_copy(q).wait()
        item_out[q * step:(q + 1) * step, :] = (kept[q] + y_in[q].astype(jnp.float32)).astype(jnp.bfloat16)
    for q in range(2 * per_block):
        core_copy(q).wait_send()
    for copy in done_copies:
        copy.wait()
    user_out[...] = done[...].reshape(width, rows).astype(jnp.float32).T.astype(jnp.bfloat16)


def hand_on(a, b, c, x, y, z):
    x[...] = a[...]
    y[...] = b[...]
    z[...] = c[...]


def solution(mesh):
    n_item = mesh.shape["item"]
    assert mesh.shape["user"] == 4

    def per_device(users, catalog_vectors, positives):
        rows, width = users.shape
        count = catalog_vectors.shape[0]
        own = count // 4
        step, tile, lanes = min(512, own), 128, 128
        per_block = own // step
        piece = width // n_item
        f32, bf16 = jnp.float32, jnp.bfloat16
        vmem = pl.BlockSpec(memory_space=pltpu.VMEM)
        dma = pltpu.SemaphoreType.DMA
        results = pl.pallas_call(
            functools.partial(kernel, n_item, step, tile, lanes),
            out_shape=(
                jax.ShapeDtypeStruct((1, rows), f32),
                jax.ShapeDtypeStruct((rows, width), bf16),
                jax.ShapeDtypeStruct((own, width), bf16),
            ),
            in_specs=[vmem] * 3,
            out_specs=(vmem,) * 3,
            scratch_shapes=[
                pltpu.VMEM((count, rows), f32),
                pltpu.VMEM((step, rows), f32),
                pltpu.VMEM((step, rows), f32),
                pltpu.VMEM((count // tile, 8, rows), f32),
                pltpu.VMEM((8, rows), f32),
                pltpu.VMEM((8, rows), f32),
                pltpu.VMEM((8, rows), f32),
                pltpu.VMEM((2, rows), f32),
                pltpu.VMEM((n_item - 1, 2, rows), f32),
                pltpu.VMEM((1, rows), f32),
                pltpu.VMEM((n_item - 1, 1, rows), f32),
                pltpu.VMEM((2, rows), f32),
                pltpu.VMEM((step, rows), bf16),
                pltpu.VMEM((step, rows), bf16),
                pltpu.VMEM((2, step, width), f32),
                pltpu.VMEM((2 * per_block, step, width), bf16),
                pltpu.VMEM((2 * per_block, step, width), bf16),
                pltpu.VMEM((per_block, step, width), bf16),
                pltpu.VMEM((per_block, step, width), bf16),
                pltpu.VMEM((per_block, step, width), f32),
                pltpu.VMEM((width, rows), f32),
                pltpu.VMEM((n_item, piece, rows), bf16),
                pltpu.VMEM((n_item - 1, piece, rows), bf16),
                pltpu.VMEM((n_item, piece, rows), bf16),
                pltpu.VMEM((rows, width), bf16),
                dma((2, n_item - 1)),
                dma((2, n_item - 1)),
                dma((2, 2 * per_block)),
                dma((2, per_block)),
                dma((2, n_item - 1)),
                dma((2, n_item - 1)),
            ],
            compiler_params=pltpu.CompilerParams(
                collective_id=0, has_side_effects=True, vmem_limit_bytes=63 * 1024 * 1024,
            ),
        )(users, catalog_vectors, positives.reshape(1, rows))
        loss, user_grad, item_grad = pl.pallas_call(
            hand_on,
            out_shape=tuple(jax.ShapeDtypeStruct(r.shape, r.dtype) for r in results),
            in_specs=[vmem] * 3,
            out_specs=(vmem,) * 3,
            compiler_params=pltpu.CompilerParams(vmem_limit_bytes=8 * 1024 * 1024),
        )(*results)
        return loss.reshape(rows), user_grad, item_grad

    in_specs = (P("user", None), P("item", None), P("user"))
    out_specs = (P("user"), P("user", None), P(("item", "user"), None))
    return jax.shard_map(
        per_device, mesh=mesh, in_specs=in_specs, out_specs=out_specs, check_vma=False
    )
```
